256 devices in a mesh: owner: 32 (over y, z_hi, x), group: 8 (over z_lo, core).
Axes of the slice: x: 4, y: 4, z: 8 (z_hi: 2, z_lo: 4; z = z_hi * 4 + z_lo), core: 2. Of those that a mesh axis runs over, the one named last changes fastest.
Arguments:
- queries: bfloat16 [128, 8192], P('group', 'owner'), may hold values from -110 to 110
- keys: bfloat16 [4, 32768, 1024], P(None, ('owner', 'group')), may hold values from -5 to 5
- values: bfloat16 [4, 32768, 1024], P(None, ('owner', 'group')), may hold values from -6 to 6
- req_doc: int32 [128, 1], replicated, may hold values from 0 to 3; in each aligned block of 16 rows (0 to 15, 16 to 31, ...) at most 8 rows name the same one
Outputs:
- attended: bfloat16 [128, 8192], P('group', 'owner')
The draws below stay inside these ranges and needn't reach their ends.
Inputs may be any that keep to these rules, and one draw needn't show every extreme that they name: `req_doc`: among the 16 requests of one group no document is read by more than 8 requests, a bound that some block reaches.
All inputs are finite; a program needn't handle non-finite values.
Results may differ from the reference program's by a relative error of at most 0.0021.
Values may be sent and summed in bfloat16 or wider, within the bound.
No kernel may reach another device: no remote copies, remote signals or barrier semaphores. Data moves between devices by JAX's collectives and lax.ppermute only.
A program may use at most 64 MiB of HBM per device.

```python
import math
import jax
import jax.numpy as jnp
import numpy as np
from jax import lax

HQ = 64
KV = 8
HD = 128
GQ = 8
DOCS = 4
TOKD = 128
R_GROUP = 16
SLOTS = 8
LEN = 32768
REQS = 128


def draw_queries(key, part):
    key = jax.random.fold_in(key, 11)
    result = 3.0 * jnp.clip(jax.random.normal(key, (REQS, HQ * HD), jnp.float32), -8.0, 8.0)
    return result.astype(jnp.bfloat16)


def draw_keys(key, part):
    key = jax.random.fold_in(key, 23)
    result = jnp.clip(jax.random.normal(key, (DOCS, LEN, KV * HD), jnp.float32), -5.0, 5.0)
    return result.astype(jnp.bfloat16)


def levels(own_key, extent, split, smallest, top_value):
    gain, own = 1.0, jax.random.fold_in(own_key, 6)
    for dim, blocks in split:
        heights = jnp.exp(jax.random.uniform(jax.random.fold_in(own, dim), (blocks,), jnp.float32, smallest / len(split), top_value / len(split)))
        gain = gain * jnp.repeat(heights, extent[dim] // blocks).reshape([-1 if axis == dim else 1 for axis in range(len(extent))])
    return gain


def deal_out(key, own, number, rows, number_of, top, limit, skew):
    sequence = jax.random.permutation(key, number_of)
    crowded, common = load_shares(number_of, rows * top, limit, skew, True), load_shares(number_of, rows * top, limit, skew, False)
    places = jnp.arange(number_of)

    def named(lengths, rotation):
        used = int((lengths > 0).sum())
        fixed = max(1, used // 4)
        passed = fixed + (places - fixed + rotation * (used - fixed)) % max(1, number_of - fixed)
        return jnp.zeros((number_of,), jnp.int32).at[sequence[jnp.where(places < fixed, places, passed)]].set(jnp.asarray(lengths, jnp.int32))

    lengths = jnp.where(number % 4 == 0, named(crowded, number // 4), named(common, number - number // 4 - 1))
    mixed = jax.random.permutation(jax.random.fold_in(own, 3), number_of)
    donor, receiver = mixed[0:number_of // 2 * 2:2], mixed[1:number_of // 2 * 2:2]
    margin = jnp.minimum(lengths[donor] - 1, limit - lengths[receiver]) // 2
    margin = jnp.where((donor == sequence[0]) | (receiver == sequence[0]) | (lengths[receiver] == 0), 0, jnp.maximum(margin, 0))
    passed = jax.random.randint(jax.random.fold_in(own, 4), (number_of // 2,), 0, 1 << 20) % (margin + 1)
    lengths = lengths.at[donor].add(-passed).at[receiver].add(passed)
    members = jnp.searchsorted(jnp.cumsum(lengths), jnp.arange(rows * top), side="right").astype(jnp.int32)
    grid = members.reshape(top, rows).T
    grid = grid[jax.random.permutation(jax.random.fold_in(own, 1), rows)]
    rotation = jax.random.randint(jax.random.fold_in(own, 2), (rows, 1), 0, top)
    return jnp.take_along_axis(grid, (jnp.arange(top)[None, :] + rotation) % top, axis=1)


def load_shares(number_of, total, most, skew, full):
    loads = [(1 << 20) // math.isqrt(standing ** skew) + 1 for standing in range(1, number_of + 1)]
    largest = most if full else min(most, max(-(-total // number_of), total * loads[0] // sum(loads)))
    least = 1 if total - largest >= number_of - 1 else 0
    holding, rest = [largest] + [least] * (number_of - 1), total - largest - least * (number_of - 1)
    while rest > 0:
        free = [i for i in range(1, number_of) if holding[i] < largest] or [i for i in range(1, number_of) if holding[i] < most]
        whole, budget = sum([loads[i] for i in free]), rest
        for i in free:
            more = min(most - holding[i], max(1, budget * loads[i] // whole), rest)
            holding[i] = holding[i] + more
            rest = rest - more
    return np.array(holding)


def bell_draw(own_key, shape, width, limit, cuts=(), dtype=jnp.bfloat16):
    entries = jax.random.normal(own_key, shape, jnp.float32) * width
    if len(cuts) > 0:
        entries = levels(own_key, shape, cuts, -0.22, 0.18) * entries
    return jnp.clip(entries, min=-limit, max=limit).astype(dtype)


def setup_inputs(seed: int = 0) -> dict:
    key_of = jax.random.split(jax.random.key(seed), 5)
    queries = draw_queries(jax.random.fold_in(key_of[4], 71), 0)
    keys = draw_keys(jax.random.fold_in(key_of[4], 71), 0)
    values = bell_draw(key_of[2], (DOCS, LEN, KV * HD), 1.0, 6.0, ((1, 256),))
    req_doc_keys = jax.random.split(jax.random.fold_in(key_of[3], 1), REQS // R_GROUP)
    req_doc_turns = jax.random.permutation(jax.random.fold_in(key_of[3], 3), REQS // R_GROUP)
    req_doc = jax.vmap(lambda own, number: deal_out(jax.random.fold_in(key_of[3], 2), own, number, R_GROUP, DOCS, 1, SLOTS, 2))(req_doc_keys, req_doc_turns).reshape((REQS, 1))
    return {"queries": queries, "keys": keys, "values": values, "req_doc": req_doc}


def reference(queries, keys, values, req_doc):
    blocks = LEN // TOKD

    def one_request(inputs):
        query, doc_index = inputs
        key_rows = lax.dynamic_index_in_dim(keys, doc_index, 0, keepdims=False)
        value_rows = lax.dynamic_index_in_dim(values, doc_index, 0, keepdims=False)
        query_f = query.astype(jnp.float32).reshape(KV, GQ, HD)
        key_f = key_rows.astype(jnp.float32).reshape(blocks, TOKD, KV, HD)
        value_f = value_rows.astype(jnp.float32).reshape(blocks, TOKD, KV, HD)
        scores = jnp.einsum('kgh,btkh->bkgt', query_f, key_f) / math.sqrt(HD)
        block_max = lax.optimization_barrier(jnp.max(scores, axis=-1))
        expo = jnp.exp(scores - block_max[..., None])
        block_sum = lax.optimization_barrier(jnp.sum(expo, axis=-1))
        weights = lax.optimization_barrier(expo.astype(jnp.bfloat16)).astype(jnp.float32)
        block_out = jnp.einsum('bkgt,btkh->bkgh', weights, value_f)
        row_max = lax.optimization_barrier(jnp.max(block_max, axis=0))
        factor = jnp.exp(block_max - row_max[None])
        total = lax.optimization_barrier(jnp.sum(factor * block_sum, axis=0))
        numer = lax.optimization_barrier(jnp.sum(factor[..., None] * block_out, axis=0))
        return (numer / total[..., None]).reshape(HQ * HD).astype(jnp.bfloat16)
    return lax.map(one_request, (queries, req_doc[:, 0].astype(jnp.int32)))
```

```python
import functools
import math

import jax
import jax.numpy as jnp
from jax import lax
from jax.experimental import pallas as pl
from jax.experimental.pallas import tpu as pltpu
from jax.sharding import PartitionSpec as P

HD = 128
DOCS = 4
TOKD = 128
ROWS = 128
R_GROUP = 16
NEAR = 8
LABELS = 32
STAT = 8
PIECE = 2 * R_GROUP + STAT
SCALE = 1.0 / math.sqrt(HD)
AXES = ("owner", "group")


def flat(y, z, x, core):
    return (((y % 4) * 2 + (z % 8) // 4) * 4 + x % 4) * 8 + (z % 4) * 2 + core


def chips():
    return [(y, z, x, c) for y in range(4) for z in range(8) for x in range(4) for c in range(2)]


def home(y, zh, x, group):
    return flat(y, 4 * zh + group - 2, x, zh)


def to_home():
    return [
        (flat(y, z, x, c), home(y, z // 4, x, (z % 4) * 2 + c)) for y, z, x, c in chips()
    ]


def home_groups():
    return [
        [home(y, zh, x, group) for x in range(4) for group in range(8)]
        for y in range(4)
        for zh in range(2)
    ]


def head_to(step, cross):
    return [(flat(y, z, x, c), flat(y + step, z, x, c ^ cross)) for y, z, x, c in chips()]


PIECES = [(step, cross) for step in range(4) for cross in range(2)]


def pack_body(keys, values, *rest):
    outs, sems = rest[:NEAR], rest[NEAR]
    owner, group = lax.axis_index("owner"), lax.axis_index("group")
    y, core = owner // 8, group % 2
    copies = []
    for place, (step, cross) in enumerate(PIECES):
        other = core if cross == 0 else 1 - core
        head = ((y + step) % 4) * 2 + other
        lanes = pl.ds(pl.multiple_of(head * HD, HD), HD)
        copies.append(
            pltpu.make_async_copy(keys.at[:, :, lanes], outs[place].at[0], sems.at[2 * place])
        )
        copies.append(
            pltpu.make_async_copy(
                values.at[:, :, lanes], outs[place].at[1], sems.at[2 * place + 1]
            )
        )
    for copy in copies:
        copy.start()
    for copy in copies:
        copy.wait()


def pack(keys, values):
    shape = jax.ShapeDtypeStruct((2, DOCS, TOKD, HD), keys.dtype)
    return pl.pallas_call(
        pack_body,
        out_shape=[shape] * NEAR,
        in_specs=[pl.BlockSpec(memory_space=pl.ANY)] * 2,
        out_specs=[pl.BlockSpec(memory_space=pl.ANY)] * NEAR,
        scratch_shapes=[pltpu.SemaphoreType.DMA((2 * NEAR,))],
        name="pack_heads",
    )(keys, values)


def attend_body(docs, queries, *rest):
    pieces, out = rest[:NEAR], rest[NEAR]
    doc = jnp.concatenate([docs[...]] * 2, axis=0)
    hot = jnp.concatenate(
        [
            jnp.broadcast_to((doc == d).astype(jnp.float32), (2 * ROWS, HD)).astype(jnp.bfloat16)
            for d in range(DOCS)
        ],
        axis=1,
    )
    lane = lax.broadcasted_iota(jnp.int32, (ROWS, HD), 1)

    def heads(pair, carry):
        both = queries[pl.ds(pair * ROWS, ROWS), :]
        rows = jnp.concatenate([both[:, :HD], both[:, HD:]], axis=0)
        wide = jnp.concatenate([rows] * DOCS, axis=1) * hot
        scores, tops = [], []
        for first in range(0, NEAR, 2):
            stretch = jnp.concatenate(
                [
                    jnp.concatenate([pieces[n][0, d] for d in range(DOCS)], axis=1)
                    for n in (first, first + 1)
                ],
                axis=0,
            )
            found = lax.dot_general(
                wide, stretch, (((1,), (1,)), ((), ())), preferred_element_type=jnp.float32
            )
            for half in (found[:, :TOKD], found[:, TOKD:]):
                scores.append(half)
                tops.append(jnp.max(half, axis=1, keepdims=True))
        top = functools.reduce(jnp.maximum, tops)
        numer = jnp.zeros((2 * ROWS, HD), jnp.float32)
        spread = jnp.zeros((2 * ROWS, TOKD), jnp.float32)
        for n in range(NEAR):
            expo = jnp.exp((scores[n] - tops[n]) * SCALE)
            factor = jnp.exp((tops[n] - top) * SCALE)
            weights = jnp.concatenate([expo.astype(jnp.bfloat16)] * DOCS, axis=1) * hot
            part = jnp.dot(
                weights,
                pieces[n][1].reshape(DOCS * TOKD, HD),
                preferred_element_type=jnp.float32,
            )
            numer = numer + part * factor
            spread = spread + expo * factor
        total = jnp.sum(spread, axis=1, keepdims=True)
        columns = jnp.where(
            lane == 0,
            top[:ROWS],
            jnp.where(
                lane == 1, top[ROWS:], jnp.where(lane == 2, total[:ROWS], total[ROWS:])
            ),
        )
        stats = columns.T[:STAT]
        for group in range(8):
            place = pair * 8 + group
            at = group * R_GROUP
            out[place, 0:R_GROUP, :] = numer[at : at + R_GROUP]
            out[place, R_GROUP : 2 * R_GROUP, :] = numer[ROWS + at : ROWS + at + R_GROUP]
            out[place, 2 * R_GROUP : PIECE, :] = stats
        return carry

    lax.fori_loop(0, 4, heads, 0)


def attend(req_doc, queries, pieces):
    return pl.pallas_call(
        attend_body,
        out_shape=jax.ShapeDtypeStruct((LABELS, PIECE, HD), jnp.float32),
        in_specs=[pl.BlockSpec(memory_space=pltpu.VMEM)] * (2 + NEAR),
        out_specs=pl.BlockSpec(memory_space=pltpu.VMEM),
        compiler_params=pltpu.CompilerParams(vmem_limit_bytes=40 * 1024 * 1024),
        name="attend_blocks",
    )(req_doc, queries, *pieces)


def merge_body(parts, out, shares):
    group = (lax.axis_index("owner") // 4 % 2) * 4 + lax.axis_index("group") // 2
    core = lax.axis_index("group") % 2
    group = (group + 2 - 4 * core + 8) % 8
    for half in range(2):
        tops = parts[:, 2 * R_GROUP + half, :]
        sums = parts[:, 2 * R_GROUP + 2 + half, :]
        top = jnp.max(tops, axis=0, keepdims=True)
        factor = jnp.exp((tops - top) * SCALE)
        share = factor / jnp.sum(factor * sums, axis=0, keepdims=True)
        padded = jnp.concatenate(
            [share, jnp.zeros((ROWS - LABELS, ROWS), jnp.float32)], axis=0
        )
        shares[...] = padded.T
        mine = shares[pl.ds(pl.multiple_of(group * R_GROUP, R_GROUP), R_GROUP), :]
        rows = slice(half * R_GROUP, (half + 1) * R_GROUP)
        acc = jnp.zeros((R_GROUP, HD), jnp.float32)
        for source in range(LABELS):
            acc = acc + mine[:, source : source + 1] * parts[source, rows, :]
        out[:, half * HD : (half + 1) * HD] = acc.astype(jnp.bfloat16)


def merge(parts):
    return pl.pallas_call(
        merge_body,
        out_shape=jax.ShapeDtypeStruct((R_GROUP, 2 * HD), jnp.bfloat16),
        in_specs=[pl.BlockSpec(memory_space=pltpu.VMEM)],
        out_specs=pl.BlockSpec(memory_space=pltpu.VMEM),
        scratch_shapes=[pltpu.VMEM((ROWS, ROWS), jnp.float32)],
        name="merge_parts",
    )(parts)


def body(queries, keys, values, req_doc):
    there = to_home()
    back = [(b, a) for a, b in there]
    groups = home_groups()
    moved = lax.ppermute(queries, AXES, there)
    own = pack(keys, values)
    pieces = [own[0]] + [
        lax.ppermute(own[n], AXES, head_to(*PIECES[n])) for n in range(1, NEAR)
    ]
    spread = jnp.broadcast_to(moved[None], (LABELS,) + moved.shape)
    gathered = lax.all_to_all(spread, AXES, 0, 0, axis_index_groups=groups, tiled=True)
    parts = attend(req_doc, gathered.reshape(LABELS * R_GROUP, 2 * HD), pieces)
    parts = lax.all_to_all(parts, AXES, 0, 0, axis_index_groups=groups, tiled=True)
    return lax.ppermute(merge(parts), AXES, back)


def solution(mesh):
    placed = (
        P("group", "owner"),
        P(None, ("owner", "group"), None),
        P(None, ("owner", "group"), None),
        P(),
    )
    return jax.shard_map(
        body, mesh=mesh, in_specs=placed, out_specs=P("group", "owner"), check_vma=False
    )
```

```python
import functools
import math

import jax
import jax.numpy as jnp
from jax import lax
from jax.experimental import pallas as pl
from jax.experimental.pallas import tpu as pltpu
from jax.sharding import PartitionSpec as P

HD = 128
DOCS = 4
TOKD = 128
ROWS = 128
R_GROUP = 16
NEAR = 8
LABELS = 32
HALF = 64
FIRST = 1 << 20
FIRST_UNROLL = 1
LAST_UNROLL = 4
ORDER = 1 << 34
STAT = 8
EARLY = 6
FINE = HALF - 3
PIECE = 3 * R_GROUP
BOX = 4 * DOCS * TOKD
SCALE = math.log2(math.e) / math.sqrt(HD)
AXES = ("owner", "group")


def flat(y, z, x, core):
    return (((y % 4) * 2 + (z % 8) // 4) * 4 + x % 4) * 8 + (z % 4) * 2 + core


def chips():
    return [(y, z, x, c) for y in range(4) for z in range(8) for x in range(4) for c in range(2)]


def planes():
    return [
        [flat(y, 4 * zh + zl, x, c) for zh in range(2) for x in range(4) for zl in range(4)]
        for y in range(4)
        for c in range(2)
    ]


def along_y(step):
    return [(flat(y, z, x, c), flat(y + step, z, x, c)) for y, z, x, c in chips()]


def other_core():
    return [(flat(y, z, x, c), flat(y, z, x, 1 - c)) for y, z, x, c in chips()]


def span(head, kind, doc):
    first = ((head * 2 + kind) * DOCS + doc) * TOKD
    return slice(first, first + TOKD)


def pack_body(keys, values, queries, docs, *rest):
    boxes, spread = rest[:4], rest[4]
    held, asked, names, sems = rest[5:]
    y = lax.axis_index("owner") // 8
    copies = [
        pltpu.make_async_copy(source.at[doc], held.at[kind, doc], sems.at[kind, doc])
        for doc in range(DOCS)
        for kind, source in enumerate((keys, values))
    ]
    copies.append(pltpu.make_async_copy(queries, asked, sems.at[2, 0]))
    copies.append(pltpu.make_async_copy(docs, names, sems.at[2, 1]))
    for copy in copies:
        copy.start()
    for n, copy in enumerate(copies[: 2 * DOCS]):
        copy.wait()
        doc, kind = n // 2, n % 2
        for step in range(4):
            for head in range(2):
                lanes = pl.ds(pl.multiple_of((((y + step) % 4) * 2 + head) * HD, HD), HD)
                boxes[step][span(head, kind, doc), :] = held[kind, doc, :, lanes]
    copies[2 * DOCS].wait()
    spread[...] = jnp.broadcast_to(asked[...][None], spread.shape)
    copies[2 * DOCS + 1].wait()
    row = names[...].astype(jnp.float32)
    boxes[0][BOX:, :] = jnp.broadcast_to(row, (R_GROUP, ROWS)).astype(jnp.bfloat16)


def pack(keys, values, queries, docs):
    kept = [
        pltpu.with_memory_space_constraint(x, pltpu.HBM) for x in (keys, values, queries, docs)
    ]
    return pl.pallas_call(
        pack_body,
        out_shape=[
            jax.ShapeDtypeStruct((BOX + extra, HD), keys.dtype) for extra in (R_GROUP, 0, 0, 0)
        ]
        + [jax.ShapeDtypeStruct((LABELS,) + queries.shape, queries.dtype)],
        in_specs=[pl.BlockSpec(memory_space=pltpu.HBM)] * 4,
        out_specs=[pl.BlockSpec(memory_space=pltpu.VMEM)] * 5,
        scratch_shapes=[
            pltpu.VMEM((2,) + keys.shape, keys.dtype),
            pltpu.VMEM(queries.shape, queries.dtype),
            pltpu.VMEM(docs.shape, docs.dtype),
            pltpu.SemaphoreType.DMA((3, DOCS)),
        ],
        compiler_params=pltpu.CompilerParams(vmem_limit_bytes=12 * 1024 * 1024),
        name="pack_heads",
    )(*kept)


def doc_mask(home, column):
    core = lax.axis_index("group") % 2
    docs = home[BOX : BOX + 1, :].astype(jnp.float32)
    column[...] = jnp.broadcast_to(docs, (ROWS, ROWS)).T
    names = [
        column[pl.ds(pl.multiple_of((2 * zl + core) * R_GROUP, R_GROUP), R_GROUP), :]
        for zl in range(4)
    ]
    doc = jnp.concatenate(names * 4, axis=0)
    return jnp.concatenate(
        [(doc == d).astype(jnp.float32).astype(jnp.bfloat16) for d in range(DOCS)], axis=1
    )


def order_body(queries, out):
    for turn in range(4):
        for half in range(2):
            rows = queries[turn * ROWS : (turn + 1) * ROWS, half * HD : (half + 1) * HD]
            out[turn, half * ROWS : (half + 1) * ROWS, :] = rows


def order(queries):
    return pl.pallas_call(
        order_body,
        out_shape=jax.ShapeDtypeStruct((4, 2 * ROWS, HD), queries.dtype),
        in_specs=[pl.BlockSpec(memory_space=pltpu.VMEM)],
        out_specs=pl.BlockSpec(memory_space=pltpu.VMEM),
        cost_estimate=pl.CostEstimate(flops=ORDER, bytes_accessed=1 << 19, transcendentals=0),
        compiler_params=pltpu.CompilerParams(vmem_limit_bytes=4 * 1024 * 1024),
        name="order_queries",
    )(queries)


def find_scores(turn, queries, boxes, hot):
    wide = jnp.concatenate([queries[turn]] * DOCS, axis=1) * hot
    scores, tops = [], []
    for left in range(0, len(boxes), 2):
        stretch = jnp.concatenate(
            [
                jnp.concatenate(
                    [part(box, turn, d * TOKD, TOKD) for d in range(DOCS)], axis=1
                )
                for box in boxes[left : left + 2]
            ],
            axis=0,
        )
        found = lax.dot_general(
            wide, stretch, (((1,), (1,)), ((), ())), preferred_element_type=jnp.float32
        )
        for one in (found[:, :TOKD], found[:, TOKD:]):
            scores.append(one)
            tops.append(jnp.max(one, axis=1, keepdims=True))
    return scores, tops


def part(box, turn, start, size):
    first = (turn // 2) * (BOX // 2)
    return box[pl.ds(pl.multiple_of(first + start, TOKD), size), :]


def add_values(turn, boxes, hot, scores, tops, top, numer):
    spread = jnp.zeros((2 * ROWS, TOKD), jnp.float32)
    for box, score, own in zip(boxes, scores, tops):
        expo = jnp.exp2((score - own) * SCALE)
        factor = jnp.exp2((own - top) * SCALE)
        weights = jnp.concatenate([expo.astype(jnp.bfloat16)] * DOCS, axis=1) * hot
        summed = jnp.dot(
            weights,
            part(box, turn, DOCS * TOKD, DOCS * TOKD),
            preferred_element_type=jnp.float32,
        )
        numer = numer + summed * factor
        spread = spread + expo * factor
    return numer, jnp.sum(spread, axis=1, keepdims=True)


def first_body(queries, *rest):
    boxes, numer_out, stat_out, column = rest[:EARLY], *rest[EARLY:]
    hot = doc_mask(boxes[0], column)
    lane = lax.broadcasted_iota(jnp.int32, (ROWS, HD), 1)

    def heads(turn, carry):
        scores, tops = find_scores(turn, queries, boxes, hot)
        top = functools.reduce(jnp.maximum, tops)
        numer, total = add_values(
            turn, boxes, hot, scores, tops, top, jnp.zeros((2 * ROWS, HD), jnp.float32)
        )
        numer_out[turn] = numer
        columns = jnp.zeros((ROWS, HD), jnp.float32)
        for place, value in enumerate((top[:ROWS], top[ROWS:], total[:ROWS], total[ROWS:])):
            columns = jnp.where(lane == place, value, columns)
        stat_out[turn] = columns.T[:STAT]
        return carry

    lax.fori_loop(0, 4, heads, 0, unroll=FIRST_UNROLL)


def attend_first(queries, boxes):
    return pl.pallas_call(
        first_body,
        out_shape=[
            jax.ShapeDtypeStruct((4, 2 * ROWS, HD), jnp.float32),
            jax.ShapeDtypeStruct((4, STAT, ROWS), jnp.float32),
        ],
        in_specs=[pl.BlockSpec(memory_space=pltpu.VMEM)] * (1 + EARLY),
        out_specs=[pl.BlockSpec(memory_space=pltpu.VMEM)] * 2,
        scratch_shapes=[pltpu.VMEM((ROWS, ROWS), jnp.float32)],
        cost_estimate=pl.CostEstimate(flops=FIRST, bytes_accessed=4 << 20, transcendentals=0),
        compiler_params=pltpu.CompilerParams(vmem_limit_bytes=16 * 1024 * 1024),
        name="attend_first",
    )(queries, *boxes)


def last_body(queries, numer_in, stat_in, home, *rest):
    boxes, out, column = rest[: NEAR - EARLY], *rest[NEAR - EARLY :]
    hot = doc_mask(home, column)
    lane = lax.broadcasted_iota(jnp.int32, (ROWS, HD), 1)

    def heads(turn, carry):
        scores, tops = find_scores(turn, queries, boxes, hot)
        padded = jnp.concatenate(
            [stat_in[turn], jnp.zeros((ROWS - STAT, ROWS), jnp.float32)], axis=0
        ).T
        old_top = jnp.concatenate([padded[:, 0:1], padded[:, 1:2]], axis=0)
        old_total = jnp.concatenate([padded[:, 2:3], padded[:, 3:4]], axis=0)
        top = functools.reduce(jnp.maximum, [old_top] + tops)
        top = top.astype(jnp.bfloat16).astype(jnp.float32)
        factor = jnp.exp2((old_top - top) * SCALE)
        numer, total = add_values(
            turn, boxes, hot, scores, tops, top, numer_in[turn] * factor
        )
        total = total + old_total * factor
        high = numer.astype(jnp.bfloat16)
        low = numer - high.astype(jnp.float32)
        total_high = total.astype(jnp.bfloat16).astype(jnp.float32)
        total_low = total - total_high
        extra = jnp.where(lane < HALF, low[:ROWS], low[ROWS:])
        for half in range(2):
            at = slice(half * ROWS, (half + 1) * ROWS)
            for place, value in enumerate((top, total_high, total_low)):
                extra = jnp.where(lane == half * HALF + FINE + place, value[at], extra)
        extra = extra.astype(jnp.bfloat16)
        for n in range(8):
            at = n * R_GROUP
            place = turn * 8 + n
            out[place, 0:R_GROUP, :] = high[at : at + R_GROUP]
            out[place, R_GROUP : 2 * R_GROUP, :] = high[ROWS + at : ROWS + at + R_GROUP]
            out[place, 2 * R_GROUP :, :] = extra[at : at + R_GROUP]
        return carry

    lax.fori_loop(0, 4, heads, 0, unroll=LAST_UNROLL)


def attend_last(queries, state, home, boxes):
    return pl.pallas_call(
        last_body,
        out_shape=jax.ShapeDtypeStruct((LABELS, PIECE, HD), jnp.bfloat16),
        in_specs=[pl.BlockSpec(memory_space=pltpu.VMEM)] * (4 + NEAR - EARLY),
        out_specs=pl.BlockSpec(memory_space=pltpu.VMEM),
        scratch_shapes=[pltpu.VMEM((ROWS, ROWS), jnp.float32)],
        compiler_params=pltpu.CompilerParams(vmem_limit_bytes=16 * 1024 * 1024),
        name="attend_last",
    )(queries, *state, home, *boxes)


def merge_body(parts, out):
    lane = lax.broadcasted_iota(jnp.int32, (R_GROUP, HD), 1)
    extras = [parts[n, 2 * R_GROUP :, :].astype(jnp.float32) for n in range(LABELS)]
    top = functools.reduce(jnp.maximum, extras)
    numer = [jnp.zeros((R_GROUP, HD), jnp.float32) for _ in range(2)]
    rest = [jnp.zeros((R_GROUP, HD), jnp.float32) for _ in range(2)]
    for n in range(LABELS):
        factors = jnp.exp2((extras[n] - top) * SCALE)
        for half in range(2):
            at = half * HALF + FINE
            factor = factors[:, at : at + 1]
            high = parts[n, half * R_GROUP : (half + 1) * R_GROUP, :].astype(jnp.float32)
            numer[half] = numer[half] + factor * high
            rest[half] = rest[half] + factor * extras[n]
    for half in range(2):
        first = half * HALF
        fine = (lane >= first) & (lane < first + FINE)
        whole = numer[half] + jnp.where(fine, rest[half], 0.0)
        sums = rest[half][:, first + FINE + 1 : first + FINE + 3]
        total = sums[:, 0:1] + sums[:, 1:2]
        out[:, half * HD : (half + 1) * HD] = (whole / total).astype(jnp.bfloat16)


def merge(parts):
    return pl.pallas_call(
        merge_body,
        out_shape=jax.ShapeDtypeStruct((R_GROUP, 2 * HD), jnp.bfloat16),
        in_specs=[pl.BlockSpec(memory_space=pltpu.VMEM)],
        out_specs=pl.BlockSpec(memory_space=pltpu.VMEM),
        name="merge_parts",
    )(parts)


def body(queries, keys, values, req_doc):
    groups = planes()
    home, *boxes, spread = pack(keys, values, queries, req_doc.reshape(1, ROWS))
    up, opposite, down = boxes
    up, down = (lax.ppermute(box, AXES, along_y(step)) for box, step in ((up, 1), (down, 3)))
    opposite, up, down = lax.optimization_barrier((opposite, up, down))
    opposite = lax.ppermute(opposite, AXES, along_y(2))
    pairs = [(box, lax.ppermute(box, AXES, other_core())) for box in (home, up, down)]
    gathered = lax.all_to_all(spread, AXES, 0, 0, axis_index_groups=groups, tiled=True)
    gathered = order(gathered.reshape(LABELS * R_GROUP, 2 * HD))
    state = attend_first(gathered, sum(pairs, ()))
    state, opposite = lax.optimization_barrier((state, opposite))
    last = (opposite, lax.ppermute(opposite, AXES, other_core()))
    parts = attend_last(gathered, state, home, last)
    parts = lax.all_to_all(parts, AXES, 0, 0, axis_index_groups=groups, tiled=True)
    return merge(parts)


def solution(mesh):
    placed = (
        P("group", "owner"),
        P(None, ("owner", "group"), None),
        P(None, ("owner", "group"), None),
        P(),
    )
    return jax.shard_map(
        body, mesh=mesh, in_specs=placed, out_specs=P("group", "owner"), check_vma=False
    )
```

```python
import functools
import math

import jax
import jax.numpy as jnp
from jax import lax
from jax.experimental import pallas as pl
from jax.experimental.pallas import tpu as pltpu
from jax.sharding import PartitionSpec as P

HD = 128
DOCS = 4
TOKD = 128
ROWS = 128
R_GROUP = 16
NEAR = 8
LABELS = 32
HALF = 64
FIRST = 1 << 20
FIRST_UNROLL = 1
LAST_UNROLL = 4
ORDER = 1 << 34
STAT = 8
EARLY = 6
FINE = HALF - 3
PIECE = 3 * R_GROUP
BOX = 4 * DOCS * TOKD
SCALE = math.log2(math.e) / math.sqrt(HD)
AXES = ("owner", "group")


def flat(y, z, x, core):
    return (((y % 4) * 2 + (z % 8) // 4) * 4 + x % 4) * 8 + (z % 4) * 2 + core


def chips():
    return [(y, z, x, c) for y in range(4) for z in range(8) for x in range(4) for c in range(2)]


def planes():
    return [
        [flat(y, 4 * zh + zl, x, c) for zh in range(2) for x in range(4) for zl in range(4)]
        for y in range(4)
        for c in range(2)
    ]


def along_y(step):
    return [(flat(y, z, x, c), flat(y + step, z, x, c)) for y, z, x, c in chips()]


def other_core():
    return [(flat(y, z, x, c), flat(y, z, x, 1 - c)) for y, z, x, c in chips()]


def span(head, kind, doc):
    first = ((head * 2 + kind) * DOCS + doc) * TOKD
    return slice(first, first + TOKD)


def pack_body(keys, values, queries, docs, *rest):
    boxes, spread = rest[:4], rest[4]
    held, asked, names, sems = rest[5:]
    y = lax.axis_index("owner") // 8
    copies = [
        pltpu.make_async_copy(source.at[doc], held.at[kind, doc], sems.at[kind, doc])
        for doc in range(DOCS)
        for kind, source in enumerate((keys, values))
    ]
    copies.append(pltpu.make_async_copy(queries, asked, sems.at[2, 0]))
    copies.append(pltpu.make_async_copy(docs, names, sems.at[2, 1]))
    for copy in copies:
        copy.start()
    for n, copy in enumerate(copies[: 2 * DOCS]):
        copy.wait()
        doc, kind = n // 2, n % 2
        for step in range(4):
            for head in range(2):
                lanes = pl.ds(pl.multiple_of((((y + step) % 4) * 2 + head) * HD, HD), HD)
                boxes[step][span(head, kind, doc), :] = held[kind, doc, :, lanes]
    copies[2 * DOCS].wait()
    spread[...] = jnp.broadcast_to(asked[...][None], spread.shape)
    copies[2 * DOCS + 1].wait()
    row = names[...].astype(jnp.float32)
    boxes[0][BOX:, :] = jnp.broadcast_to(row, (R_GROUP, ROWS)).astype(jnp.bfloat16)


def pack(keys, values, queries, docs):
    kept = [
        pltpu.with_memory_space_constraint(x, pltpu.HBM) for x in (keys, values, queries, docs)
    ]
    return pl.pallas_call(
        pack_body,
        out_shape=[
            jax.ShapeDtypeStruct((BOX + extra, HD), keys.dtype) for extra in (R_GROUP, 0, 0, 0)
        ]
        + [jax.ShapeDtypeStruct((LABELS,) + queries.shape, queries.dtype)],
        in_specs=[pl.BlockSpec(memory_space=pltpu.HBM)] * 4,
        out_specs=[pl.BlockSpec(memory_space=pltpu.VMEM)] * 5,
        scratch_shapes=[
            pltpu.VMEM((2,) + keys.shape, keys.dtype),
            pltpu.VMEM(queries.shape, queries.dtype),
            pltpu.VMEM(docs.shape, docs.dtype),
            pltpu.SemaphoreType.DMA((3, DOCS)),
        ],
        compiler_params=pltpu.CompilerParams(vmem_limit_bytes=12 * 1024 * 1024),
        name="pack_heads",
    )(*kept)


def doc_mask(home, column):
    core = lax.axis_index("group") % 2
    docs = home[BOX:, :].astype(jnp.float32)[:1]
    column[...] = jnp.broadcast_to(docs, (ROWS, ROWS)).T
    names = [
        column[pl.ds(pl.multiple_of((2 * zl + core) * R_GROUP, R_GROUP), R_GROUP), :]
        for zl in range(4)
    ]
    doc = jnp.concatenate(names * 4, axis=0)
    return jnp.concatenate(
        [(doc == d).astype(jnp.float32).astype(jnp.bfloat16) for d in range(DOCS)], axis=1
    )


def order_body(queries, out):
    for turn in range(4):
        for half in range(2):
            rows = queries[turn * ROWS : (turn + 1) * ROWS, half * HD : (half + 1) * HD]
            out[turn, half * ROWS : (half + 1) * ROWS, :] = rows


def order(queries):
    return pl.pallas_call(
        order_body,
        out_shape=jax.ShapeDtypeStruct((4, 2 * ROWS, HD), queries.dtype),
        in_specs=[pl.BlockSpec(memory_space=pltpu.VMEM)],
        out_specs=pl.BlockSpec(memory_space=pltpu.VMEM),
        cost_estimate=pl.CostEstimate(flops=ORDER, bytes_accessed=1 << 19, transcendentals=0),
        compiler_params=pltpu.CompilerParams(vmem_limit_bytes=4 * 1024 * 1024),
        name="order_queries",
    )(queries)


def find_scores(turn, queries, boxes, hot):
    wide = jnp.concatenate([queries[turn]] * DOCS, axis=1) * hot
    scores, tops = [], []
    for left in range(0, len(boxes), 2):
        stretch = jnp.concatenate(
            [
                jnp.concatenate(
                    [part(box, turn, d * TOKD, TOKD) for d in range(DOCS)], axis=1
                )
                for box in boxes[left : left + 2]
            ],
            axis=0,
        )
        found = lax.dot_general(
            wide, stretch, (((1,), (1,)), ((), ())), preferred_element_type=jnp.float32
        )
        for one in (found[:, :TOKD], found[:, TOKD:]):
            scores.append(one)
            tops.append(jnp.max(one, axis=1, keepdims=True))
    return scores, tops


def part(box, turn, start, size):
    first = (turn // 2) * (BOX // 2)
    return box[pl.ds(pl.multiple_of(first + start, TOKD), size), :]


def add_values(turn, boxes, hot, scores, tops, top, numer):
    spread = jnp.zeros((2 * ROWS, TOKD), jnp.float32)
    for box, score, own in zip(boxes, scores, tops):
        expo = jnp.exp2((score - own) * SCALE)
        factor = jnp.exp2((own - top) * SCALE)
        weights = jnp.concatenate([expo.astype(jnp.bfloat16)] * DOCS, axis=1) * hot
        summed = jnp.dot(
            weights,
            part(box, turn, DOCS * TOKD, DOCS * TOKD),
            preferred_element_type=jnp.float32,
        )
        numer = numer + summed * factor
        spread = spread + expo * factor
    return numer, jnp.sum(spread, axis=1, keepdims=True)


def first_body(queries, *rest):
    boxes, numer_out, stat_out, column = rest[:EARLY], *rest[EARLY:]
    hot = doc_mask(boxes[0], column)
    lane = lax.broadcasted_iota(jnp.int32, (ROWS, HD), 1)

    def heads(turn, carry):
        scores, tops = find_scores(turn, queries, boxes, hot)
        top = functools.reduce(jnp.maximum, tops)
        numer, total = add_values(
            turn, boxes, hot, scores, tops, top, jnp.zeros((2 * ROWS, HD), jnp.float32)
        )
        numer_out[turn] = numer
        columns = jnp.zeros((ROWS, HD), jnp.float32)
        for place, value in enumerate((top[:ROWS], top[ROWS:], total[:ROWS], total[ROWS:])):
            columns = jnp.where(lane == place, value, columns)
        stat_out[turn] = columns.T[:STAT]
        return carry

    lax.fori_loop(0, 4, heads, 0, unroll=FIRST_UNROLL)


def attend_first(queries, boxes):
    return pl.pallas_call(
        first_body,
        out_shape=[
            jax.ShapeDtypeStruct((4, 2 * ROWS, HD), jnp.float32),
            jax.ShapeDtypeStruct((4, STAT, ROWS), jnp.float32),
        ],
        in_specs=[pl.BlockSpec(memory_space=pltpu.VMEM)] * (1 + EARLY),
        out_specs=[pl.BlockSpec(memory_space=pltpu.VMEM)] * 2,
        scratch_shapes=[pltpu.VMEM((ROWS, ROWS), jnp.float32)],
        cost_estimate=pl.CostEstimate(flops=FIRST, bytes_accessed=4 << 20, transcendentals=0),
        compiler_params=pltpu.CompilerParams(vmem_limit_bytes=16 * 1024 * 1024),
        name="attend_first",
    )(queries, *boxes)


def last_body(queries, numer_in, stat_in, home, *rest):
    boxes, out, column = rest[: NEAR - EARLY], *rest[NEAR - EARLY :]
    hot = doc_mask(home, column)
    lane = lax.broadcasted_iota(jnp.int32, (ROWS, HD), 1)

    def heads(turn, carry):
        scores, tops = find_scores(turn, queries, boxes, hot)
        padded = jnp.concatenate(
            [stat_in[turn], jnp.zeros((ROWS - STAT, ROWS), jnp.float32)], axis=0
        ).T
        old_top = jnp.concatenate([padded[:, 0:1], padded[:, 1:2]], axis=0)
        old_total = jnp.concatenate([padded[:, 2:3], padded[:, 3:4]], axis=0)
        top = functools.reduce(jnp.maximum, [old_top] + tops)
        top = top.astype(jnp.bfloat16).astype(jnp.float32)
        factor = jnp.exp2((old_top - top) * SCALE)
        numer, total = add_values(
            turn, boxes, hot, scores, tops, top, numer_in[turn] * factor
        )
        total = total + old_total * factor
        high = numer.astype(jnp.bfloat16)
        low = numer - high.astype(jnp.float32)
        total_high = total.astype(jnp.bfloat16).astype(jnp.float32)
        total_low = total - total_high
        extra = jnp.where(lane < HALF, low[:ROWS], low[ROWS:])
        for half in range(2):
            at = slice(half * ROWS, (half + 1) * ROWS)
            for place, value in enumerate((top, total_high, total_low)):
                extra = jnp.where(lane == half * HALF + FINE + place, value[at], extra)
        extra = extra.astype(jnp.bfloat16)
        for n in range(8):
            at = n * R_GROUP
            place = turn * 8 + n
            out[place, 0:R_GROUP, :] = high[at : at + R_GROUP]
            out[place, R_GROUP : 2 * R_GROUP, :] = high[ROWS + at : ROWS + at + R_GROUP]
            out[place, 2 * R_GROUP :, :] = extra[at : at + R_GROUP]
        return carry

    lax.fori_loop(0, 4, heads, 0, unroll=LAST_UNROLL)


def attend_last(queries, state, home, boxes):
    return pl.pallas_call(
        last_body,
        out_shape=jax.ShapeDtypeStruct((LABELS, PIECE, HD), jnp.bfloat16),
        in_specs=[pl.BlockSpec(memory_space=pltpu.VMEM)] * (4 + NEAR - EARLY),
        out_specs=pl.BlockSpec(memory_space=pltpu.VMEM),
        scratch_shapes=[pltpu.VMEM((ROWS, ROWS), jnp.float32)],
        compiler_params=pltpu.CompilerParams(vmem_limit_bytes=16 * 1024 * 1024),
        name="attend_last",
    )(queries, *state, home, *boxes)


def merge_body(parts, out):
    lane = lax.broadcasted_iota(jnp.int32, (R_GROUP, HD), 1)
    extras = [parts[n, 2 * R_GROUP :, :].astype(jnp.float32) for n in range(LABELS)]
    top = functools.reduce(jnp.maximum, extras)
    numer = [jnp.zeros((R_GROUP, HD), jnp.float32) for _ in range(2)]
    rest = [jnp.zeros((R_GROUP, HD), jnp.float32) for _ in range(2)]
    for n in range(LABELS):
        factors = jnp.exp2((extras[n] - top) * SCALE)
        for half in range(2):
            at = half * HALF + FINE
            factor = factors[:, at : at + 1]
            high = parts[n, half * R_GROUP : (half + 1) * R_GROUP, :].astype(jnp.float32)
            numer[half] = numer[half] + factor * high
            rest[half] = rest[half] + factor * extras[n]
    for half in range(2):
        first = half * HALF
        fine = (lane >= first) & (lane < first + FINE)
        whole = numer[half] + jnp.where(fine, rest[half], 0.0)
        sums = rest[half][:, first + FINE + 1 : first + FINE + 3]
        total = sums[:, 0:1] + sums[:, 1:2]
        out[:, half * HD : (half + 1) * HD] = (whole / total).astype(jnp.bfloat16)


def merge(parts):
    return pl.pallas_call(
        merge_body,
        out_shape=jax.ShapeDtypeStruct((R_GROUP, 2 * HD), jnp.bfloat16),
        in_specs=[pl.BlockSpec(memory_space=pltpu.VMEM)],
        out_specs=pl.BlockSpec(memory_space=pltpu.VMEM),
        name="merge_parts",
    )(pltpu.with_memory_space_constraint(parts, pltpu.VMEM))


def body(queries, keys, values, req_doc):
    groups = planes()
    home, *boxes, spread = pack(keys, values, queries, req_doc.reshape(1, ROWS))
    up, opposite, down = boxes
    up, down = (lax.ppermute(box, AXES, along_y(step)) for box, step in ((up, 1), (down, 3)))
    opposite, up = lax.optimization_barrier((opposite, up))
    opposite = lax.ppermute(opposite, AXES, along_y(2))
    pairs = [(box, lax.ppermute(box, AXES, other_core())) for box in (home, up, down)]
    gathered = lax.all_to_all(spread, AXES, 0, 0, axis_index_groups=groups, tiled=True)
    gathered = order(gathered.reshape(LABELS * R_GROUP, 2 * HD))
    state = attend_first(gathered, sum(pairs, ()))
    state, opposite = lax.optimization_barrier((state, opposite))
    last = (opposite, lax.ppermute(opposite, AXES, other_core()))
    parts = attend_last(gathered, state, home, last)
    parts = lax.all_to_all(parts, AXES, 0, 0, axis_index_groups=groups, tiled=True)
    return merge(parts)


def solution(mesh):
    placed = (
        P("group", "owner"),
        P(None, ("owner", "group"), None),
        P(None, ("owner", "group"), None),
        P(),
    )
    return jax.shard_map(
        body, mesh=mesh, in_specs=placed, out_specs=P("group", "owner"), check_vma=False
    )
```

```python
import functools
import math

import jax
import jax.numpy as jnp
from jax import lax
from jax.experimental import pallas as pl
from jax.experimental.pallas import tpu as pltpu
from jax.sharding import PartitionSpec as P

HD = 128
DOCS = 4
TOKD = 128
ROWS = 128
R_GROUP = 16
NEAR = 8
LABELS = 32
HALF = 64
FIRST = 1 << 20
FIRST_UNROLL = 1
LAST_UNROLL = 4
ORDER = 1 << 34
STAT = 8
EARLY = 6
FINE = HALF - 3
PIECE = 3 * R_GROUP
BOX = 4 * DOCS * TOKD
SCALE = math.log2(math.e) / math.sqrt(HD)
AXES = ("owner", "group")


def flat(y, z, x, core):
    return (((y % 4) * 2 + (z % 8) // 4) * 4 + x % 4) * 8 + (z % 4) * 2 + core


def chips():
    return [(y, z, x, c) for y in range(4) for z in range(8) for x in range(4) for c in range(2)]


def planes():
    return [
        [flat(y, 4 * zh + zl, x, c) for zl in range(4) for zh in range(2) for x in range(4)]
        for y in range(4)
        for c in range(2)
    ]


def along_y(step):
    return [(flat(y, z, x, c), flat(y + step, z, x, c)) for y, z, x, c in chips()]


def other_core():
    return [(flat(y, z, x, c), flat(y, z, x, 1 - c)) for y, z, x, c in chips()]


def span(head, kind, doc):
    first = ((head * 2 + kind) * DOCS + doc) * TOKD
    return slice(first, first + TOKD)


def pack_body(keys, values, queries, docs, *rest):
    boxes, spread = rest[:4], rest[4]
    held, asked, names, sems = rest[5:]
    y = lax.axis_index("owner") // 8
    copies = [
        pltpu.make_async_copy(source.at[doc], held.at[kind, doc], sems.at[kind, doc])
        for doc in range(DOCS)
        for kind, source in enumerate((keys, values))
    ]
    copies.append(pltpu.make_async_copy(queries, asked, sems.at[2, 0]))
    copies.append(pltpu.make_async_copy(docs, names, sems.at[2, 1]))
    for copy in copies:
        copy.start()
    for n, copy in enumerate(copies[: 2 * DOCS]):
        copy.wait()
        doc, kind = n // 2, n % 2
        for step in range(4):
            for head in range(2):
                lanes = pl.ds(pl.multiple_of((((y + step) % 4) * 2 + head) * HD, HD), HD)
                boxes[step][span(head, kind, doc), :] = held[kind, doc, :, lanes]
    copies[2 * DOCS].wait()
    spread[...] = jnp.broadcast_to(asked[...][None], spread.shape)
    copies[2 * DOCS + 1].wait()
    row = names[...].astype(jnp.float32)
    boxes[0][BOX:, :] = jnp.broadcast_to(row, (R_GROUP, ROWS)).astype(jnp.bfloat16)


def pack(keys, values, queries, docs):
    kept = [
        pltpu.with_memory_space_constraint(x, pltpu.HBM) for x in (keys, values, queries, docs)
    ]
    return pl.pallas_call(
        pack_body,
        out_shape=[
            jax.ShapeDtypeStruct((BOX + extra, HD), keys.dtype) for extra in (R_GROUP, 0, 0, 0)
        ]
        + [jax.ShapeDtypeStruct((LABELS,) + queries.shape, queries.dtype)],
        in_specs=[pl.BlockSpec(memory_space=pltpu.HBM)] * 4,
        out_specs=[pl.BlockSpec(memory_space=pltpu.VMEM)] * 5,
        scratch_shapes=[
            pltpu.VMEM((2,) + keys.shape, keys.dtype),
            pltpu.VMEM(queries.shape, queries.dtype),
            pltpu.VMEM(docs.shape, docs.dtype),
            pltpu.SemaphoreType.DMA((3, DOCS)),
        ],
        compiler_params=pltpu.CompilerParams(vmem_limit_bytes=12 * 1024 * 1024),
        name="pack_heads",
    )(*kept)


def doc_mask(home, column):
    core = lax.axis_index("group") % 2
    docs = home[BOX:, :].astype(jnp.float32)[:1]
    column[...] = jnp.broadcast_to(docs, (ROWS, ROWS)).T
    names = [
        column[pl.ds(pl.multiple_of((2 * zl + core) * R_GROUP, R_GROUP), R_GROUP), :]
        for zl in range(4)
    ]
    doc = jnp.concatenate(names * 4, axis=0)
    return jnp.concatenate(
        [(doc == d).astype(jnp.float32).astype(jnp.bfloat16) for d in range(DOCS)], axis=1
    )


def order_body(queries, out):
    for turn in range(4):
        for n in range(8):
            place = (n % 4) * 8 + (turn // 2) * 4 + (turn % 2) * 2 + n // 4
            block = queries[place * R_GROUP : (place + 1) * R_GROUP, :]
            for half in range(2):
                at = half * ROWS + n * R_GROUP
                out[turn, at : at + R_GROUP, :] = block[:, half * HD : (half + 1) * HD]


def order(queries):
    return pl.pallas_call(
        order_body,
        out_shape=jax.ShapeDtypeStruct((4, 2 * ROWS, HD), queries.dtype),
        in_specs=[pl.BlockSpec(memory_space=pltpu.VMEM)],
        out_specs=pl.BlockSpec(memory_space=pltpu.VMEM),
        cost_estimate=pl.CostEstimate(flops=ORDER, bytes_accessed=1 << 19, transcendentals=0),
        compiler_params=pltpu.CompilerParams(vmem_limit_bytes=4 * 1024 * 1024),
        name="order_queries",
    )(queries)


def find_scores(turn, queries, boxes, hot):
    wide = jnp.concatenate([queries[turn]] * DOCS, axis=1) * hot
    scores, tops = [], []
    for left in range(0, len(boxes), 2):
        stretch = jnp.concatenate(
            [
                jnp.concatenate(
                    [part(box, turn, d * TOKD, TOKD) for d in range(DOCS)], axis=1
                )
                for box in boxes[left : left + 2]
            ],
            axis=0,
        )
        found = lax.dot_general(
            wide, stretch, (((1,), (1,)), ((), ())), preferred_element_type=jnp.float32
        )
        for one in (found[:, :TOKD], found[:, TOKD:]):
            scores.append(one)
            tops.append(jnp.max(one, axis=1, keepdims=True))
    return scores, tops


def part(box, turn, start, size):
    first = (turn // 2) * (BOX // 2)
    return box[pl.ds(pl.multiple_of(first + start, TOKD), size), :]


def add_values(turn, boxes, hot, scores, tops, top, numer):
    spread = jnp.zeros((2 * ROWS, TOKD), jnp.float32)
    for box, score, own in zip(boxes, scores, tops):
        expo = jnp.exp2((score - own) * SCALE)
        factor = jnp.exp2((own - top) * SCALE)
        weights = jnp.concatenate([expo.astype(jnp.bfloat16)] * DOCS, axis=1) * hot
        summed = jnp.dot(
            weights,
            part(box, turn, DOCS * TOKD, DOCS * TOKD),
            preferred_element_type=jnp.float32,
        )
        numer = numer + summed * factor
        spread = spread + expo * factor
    return numer, jnp.sum(spread, axis=1, keepdims=True)


def first_body(queries, *rest):
    boxes, numer_out, stat_out, column = rest[:EARLY], *rest[EARLY:]
    hot = doc_mask(boxes[0], column)
    lane = lax.broadcasted_iota(jnp.int32, (ROWS, HD), 1)

    def heads(turn, carry):
        scores, tops = find_scores(turn, queries, boxes, hot)
        top = functools.reduce(jnp.maximum, tops)
        numer, total = add_values(
            turn, boxes, hot, scores, tops, top, jnp.zeros((2 * ROWS, HD), jnp.float32)
        )
        numer_out[turn] = numer
        columns = jnp.zeros((ROWS, HD), jnp.float32)
        for place, value in enumerate((top[:ROWS], top[ROWS:], total[:ROWS], total[ROWS:])):
            columns = jnp.where(lane == place, value, columns)
        stat_out[turn] = columns.T[:STAT]
        return carry

    lax.fori_loop(0, 4, heads, 0, unroll=FIRST_UNROLL)


def attend_first(queries, boxes):
    return pl.pallas_call(
        first_body,
        out_shape=[
            jax.ShapeDtypeStruct((4, 2 * ROWS, HD), jnp.float32),
            jax.ShapeDtypeStruct((4, STAT, ROWS), jnp.float32),
        ],
        in_specs=[pl.BlockSpec(memory_space=pltpu.VMEM)] * (1 + EARLY),
        out_specs=[pl.BlockSpec(memory_space=pltpu.VMEM)] * 2,
        scratch_shapes=[pltpu.VMEM((ROWS, ROWS), jnp.float32)],
        cost_estimate=pl.CostEstimate(flops=FIRST, bytes_accessed=4 << 20, transcendentals=0),
        compiler_params=pltpu.CompilerParams(vmem_limit_bytes=16 * 1024 * 1024),
        name="attend_first",
    )(queries, *boxes)


def last_body(queries, numer_in, stat_in, home, *rest):
    boxes, out, column = rest[: NEAR - EARLY], *rest[NEAR - EARLY :]
    hot = doc_mask(home, column)
    lane = lax.broadcasted_iota(jnp.int32, (ROWS, HD), 1)

    def heads(turn, carry):
        scores, tops = find_scores(turn, queries, boxes, hot)
        padded = jnp.concatenate(
            [stat_in[turn], jnp.zeros((ROWS - STAT, ROWS), jnp.float32)], axis=0
        ).T
        old_top = jnp.concatenate([padded[:, 0:1], padded[:, 1:2]], axis=0)
        old_total = jnp.concatenate([padded[:, 2:3], padded[:, 3:4]], axis=0)
        top = functools.reduce(jnp.maximum, [old_top] + tops)
        top = top.astype(jnp.bfloat16).astype(jnp.float32)
        factor = jnp.exp2((old_top - top) * SCALE)
        numer, total = add_values(
            turn, boxes, hot, scores, tops, top, numer_in[turn] * factor
        )
        total = total + old_total * factor
        high = numer.astype(jnp.bfloat16)
        low = numer - high.astype(jnp.float32)
        total_high = total.astype(jnp.bfloat16).astype(jnp.float32)
        total_low = total - total_high
        extra = jnp.where(lane < HALF, low[:ROWS], low[ROWS:])
        for half in range(2):
            at = slice(half * ROWS, (half + 1) * ROWS)
            for place, value in enumerate((top, total_high, total_low)):
                extra = jnp.where(lane == half * HALF + FINE + place, value[at], extra)
        extra = extra.astype(jnp.bfloat16)
        for n in range(8):
            at = n * R_GROUP
            place = (n % 4) * 8 + (turn // 2) * 4 + (turn % 2) * 2 + n // 4
            out[place, 0:R_GROUP, :] = high[at : at + R_GROUP]
            out[place, R_GROUP : 2 * R_GROUP, :] = high[ROWS + at : ROWS + at + R_GROUP]
            out[place, 2 * R_GROUP :, :] = extra[at : at + R_GROUP]
        return carry

    lax.fori_loop(0, 4, heads, 0, unroll=LAST_UNROLL)


def attend_last(queries, state, home, boxes):
    return pl.pallas_call(
        last_body,
        out_shape=jax.ShapeDtypeStruct((LABELS, PIECE, HD), jnp.bfloat16),
        in_specs=[pl.BlockSpec(memory_space=pltpu.VMEM)] * (4 + NEAR - EARLY),
        out_specs=pl.BlockSpec(memory_space=pltpu.VMEM),
        scratch_shapes=[pltpu.VMEM((ROWS, ROWS), jnp.float32)],
        compiler_params=pltpu.CompilerParams(vmem_limit_bytes=16 * 1024 * 1024),
        name="attend_last",
    )(queries, *state, home, *boxes)


def merge_body(parts, out):
    lane = lax.broadcasted_iota(jnp.int32, (R_GROUP, HD), 1)
    extras = [parts[n, 2 * R_GROUP :, :].astype(jnp.float32) for n in range(LABELS)]
    top = functools.reduce(jnp.maximum, extras)
    numer = [jnp.zeros((R_GROUP, HD), jnp.float32) for _ in range(2)]
    rest = [jnp.zeros((R_GROUP, HD), jnp.float32) for _ in range(2)]
    for n in range(LABELS):
        factors = jnp.exp2((extras[n] - top) * SCALE)
        for half in range(2):
            at = half * HALF + FINE
            factor = factors[:, at : at + 1]
            high = parts[n, half * R_GROUP : (half + 1) * R_GROUP, :].astype(jnp.float32)
            numer[half] = numer[half] + factor * high
            rest[half] = rest[half] + factor * extras[n]
    for half in range(2):
        first = half * HALF
        fine = (lane >= first) & (lane < first + FINE)
        whole = numer[half] + jnp.where(fine, rest[half], 0.0)
        sums = rest[half][:, first + FINE + 1 : first + FINE + 3]
        total = sums[:, 0:1] + sums[:, 1:2]
        out[:, half * HD : (half + 1) * HD] = (whole / total).astype(jnp.bfloat16)


def merge(parts):
    return pl.pallas_call(
        merge_body,
        out_shape=jax.ShapeDtypeStruct((R_GROUP, 2 * HD), jnp.bfloat16),
        in_specs=[pl.BlockSpec(memory_space=pltpu.VMEM)],
        out_specs=pl.BlockSpec(memory_space=pltpu.VMEM),
        name="merge_parts",
    )(pltpu.with_memory_space_constraint(parts, pltpu.VMEM))


def body(queries, keys, values, req_doc):
    groups = planes()
    home, *boxes, spread = pack(keys, values, queries, req_doc.reshape(1, ROWS))
    up, opposite, down = boxes
    up, down = (lax.ppermute(box, AXES, along_y(step)) for box, step in ((up, 1), (down, 3)))
    opposite, up = lax.optimization_barrier((opposite, up))
    opposite = lax.ppermute(opposite, AXES, along_y(2))
    pairs = [(box, lax.ppermute(box, AXES, other_core())) for box in (home, up, down)]
    gathered = lax.all_to_all(spread, AXES, 0, 0, axis_index_groups=groups, tiled=True)
    gathered = order(gathered.reshape(LABELS * R_GROUP, 2 * HD))
    state = attend_first(gathered, sum(pairs, ()))
    state, opposite = lax.optimization_barrier((state, opposite))
    last = (opposite, lax.ppermute(opposite, AXES, other_core()))
    parts = attend_last(gathered, state, home, last)
    parts = lax.all_to_all(parts, AXES, 0, 0, axis_index_groups=groups, tiled=True)
    return merge(parts)


def solution(mesh):
    placed = (
        P("group", "owner"),
        P(None, ("owner", "group"), None),
        P(None, ("owner", "group"), None),
        P(),
    )
    return jax.shard_map(
        body, mesh=mesh, in_specs=placed, out_specs=P("group", "owner"), check_vma=False
    )
```
